32 devices in a mesh: grp: 2 (over x), lon: 16 (over z, y, core).
Axes of the slice: x: 2, y: 2, z: 4, core: 2. Of those that a mesh axis runs over, the one named last changes fastest.
Arguments:
- tracers: float32 [2, 2, 16, 64, 2048], P('grp', None, None, None, 'lon'), parts along dimension 0, may hold values from -6 to 6
- east_velocity: float32 [2, 16, 64, 2048], P('grp', None, None, 'lon'), parts along dimension 0, may hold values from -1 to 1
- north_velocity: float32 [2, 16, 64, 2048], P('grp', None, None, 'lon'), parts along dimension 0, may hold values from -1 to 1
- forcing: float32 [2, 64, 2048], P('grp', None, 'lon'), parts along dimension 0, may hold values from -6 to 6
- levels_wet: int32 [64, 2048], P(None, 'lon'), may hold values from 0 to 16, as said below
- closure_in: float32 [64, 4], replicated, may hold values from -3 to 3
- closure_out: float32 [15, 64], replicated, may hold values from -0.75 to 0.75
Outputs:
- tracers_out: float32 [2, 2, 16, 64, 2048], P('grp', None, None, None, 'lon'), parts along dimension 0
- surface: float32 [2, 64, 2048], P('grp', None, 'lon'), parts along dimension 0
The draws below stay inside these ranges and needn't reach their ends.
There are 2 independent parts, one for each index of `grp`. The reference program is written for one: setup_inputs(seed, part) draws one part's arguments, and reference() takes and returns one part's arrays. A program takes and returns all parts, laid end to end along the dimension named above; an argument that names none is the same for every part. Nothing has to cross between parts.
Inputs may be any that keep to these rules, and one draw needn't show every extreme that they name: `levels_wet`: the globe is cut into tiles of a quarter of 64 rows by half of 128 columns; a land tile is 0 throughout, and elsewhere a column has 8 to 16 wet levels.
All inputs are finite; a program needn't handle non-finite values.
Results may differ from the reference program's by a relative error of at most 0.00019.
Values sent between devices are 32-bit elements; how exact they have to be, the bound alone decides.
A program may use at most 64 MiB of HBM per device.

```python
import jax
import jax.numpy as jnp
from jax import lax

MEMBERS = 1
CX = 128
NY = 64
NZ = 16
STEPS = 3
SUB = 3
ITERS = 8
HID = 64
FEAT = 4
NX = 2048


def draw_levels_wet(key, part):
    key = jax.random.fold_in(key, 11)
    tile_key, depth_key = jax.random.split(key)
    tile_rows = NY // 4
    tile_cols = CX // 2
    land = jax.random.randint(tile_key, (4, NX // tile_cols), 0, 10) < 3
    land = land.at[0, 0].set(True)
    land = land.at[3, NX // tile_cols - 1].set(False)
    depth = jax.random.randint(depth_key, (NY, NX), NZ // 2, NZ + 1)
    depth = depth.at[NY - 1, NX - 1].set(NZ)
    cell_land = jnp.repeat(jnp.repeat(land, tile_rows, axis=0), tile_cols, axis=1)
    return jnp.where(cell_land, 0, depth).astype(jnp.int32)


def shard_levels(key, extent, cuts, smallest, top_value):
    gain, own = 1.0, jax.random.fold_in(key, 6)
    for position, blocks in cuts:
        draws = jnp.exp(jax.random.uniform(jax.random.fold_in(own, position), (blocks,), jnp.float32, smallest / len(cuts), top_value / len(cuts)))
        gain = gain * jnp.repeat(draws, extent[position] // blocks).reshape([-1 if axis == position else 1 for axis in range(len(extent))])
    return gain


def scatter_about(stream_key, dims, scale, most, shards=(), kind=jnp.bfloat16):
    values = jax.random.normal(stream_key, dims, jnp.float32) * scale
    if len(shards) > 0:
        values = shard_levels(stream_key, dims, shards, -0.22, 0.18) * values
    return jnp.clip(values, min=-most, max=most).astype(kind)


def setup_inputs(seed: int = 0, part: int = 0) -> dict:
    seeds = jax.random.split(jax.random.key(seed), 8)
    part_splits = jax.random.split(jax.random.fold_in(seeds[7], part), 8)
    return {
        "tracers": scatter_about(part_splits[0], (MEMBERS, 2, NZ, NY, NX), 1.0, 6.0, ((4, 16),), jnp.float32),
        "east_velocity": jnp.clip(jax.random.uniform(part_splits[1], (MEMBERS, NZ, NY, NX), jnp.float32, -1.0, 1.0) * shard_levels(part_splits[1], (MEMBERS, NZ, NY, NX), ((3, 16),), -0.4, 0.0), -1.0, 1.0),
        "north_velocity": jnp.clip(jax.random.uniform(part_splits[2], (MEMBERS, NZ, NY, NX), jnp.float32, -1.0, 1.0) * shard_levels(part_splits[2], (MEMBERS, NZ, NY, NX), ((3, 16),), -0.4, 0.0), -1.0, 1.0),
        "forcing": scatter_about(part_splits[3], (MEMBERS, NY, NX), 1.0, 6.0, ((2, 16),), jnp.float32),
        "levels_wet": draw_levels_wet(jax.random.fold_in(seeds[7], 71), part),
        "closure_in": scatter_about(seeds[5], (HID, FEAT), FEAT ** -0.5, 3.0, (), jnp.float32),
        "closure_out": scatter_about(seeds[6], (NZ - 1, HID), HID ** -0.5, 0.75, (), jnp.float32),
    }


C_ADV = 0.25
KMIN = 0.05
DTV = 2.0
SIG = 0.1
GRAV = 0.1


def periodic(field, width):
    return jnp.concatenate([field[..., -width:], field, field[..., :width]], axis=-1)


def upwind_flux(vel, tm1, t0, t1, t2):
    return vel * (7.0 * (t0 + t1) - (tm1 + t2)) / 12.0 - jnp.abs(vel) * (3.0 * (t1 - t0) - (t2 - tm1)) / 12.0


def advect(tr_ext, u_ext, v_mid, wet_ext):
    length = tr_ext.shape[-1]
    flux = upwind_flux(u_ext[..., 1:length - 2], tr_ext[..., 0:length - 3], tr_ext[..., 1:length - 2],
                       tr_ext[..., 2:length - 1], tr_ext[..., 3:length])
    flux = flux * (wet_ext[..., 1:length - 2] * wet_ext[..., 2:length - 1])
    zonal = flux[..., 1:] - flux[..., :-1]
    centre = tr_ext[..., 2:length - 2]
    wet_mid = wet_ext[..., 2:length - 2]
    rows = centre.shape[-2]
    padded = jnp.pad(centre, ((0, 0), (0, 0), (2, 2), (0, 0)))
    wet_pad = jnp.pad(wet_mid, ((0, 0), (2, 2), (0, 0)))
    face_v = jnp.pad(v_mid, ((0, 0), (1, 0), (0, 0)))
    gflux = upwind_flux(face_v, padded[..., 0:rows + 1, :], padded[..., 1:rows + 2, :],
                        padded[..., 2:rows + 3, :], padded[..., 3:rows + 4, :])
    gflux = gflux * (wet_pad[:, 1:rows + 2, :] * wet_pad[:, 2:rows + 3, :])
    merid = gflux[..., 1:, :] - gflux[..., :-1, :]
    return (centre - C_ADV * (zonal + merid)) * wet_mid


def closure_mix(tracer, wet, closure_in, closure_out):
    levels = tracer.shape[1]
    feats = jnp.stack([tracer[0, 0], tracer[1, 0], jnp.sum(tracer[0], axis=0) / levels,
                       jnp.sum(tracer[1], axis=0) / levels], axis=0)
    hidden = jnp.tanh(jnp.einsum('hf,fyx->hyx', closure_in, feats, precision=lax.Precision.HIGHEST))
    score = jnp.einsum('kh,hyx->kyx', closure_out, hidden, precision=lax.Precision.HIGHEST)
    kappa = (KMIN + jax.nn.softplus(score)) * wet[1:]
    lower = [None] + [-DTV * kappa[k - 1] for k in range(1, levels)]
    upper = [-DTV * kappa[k] for k in range(levels - 1)] + [None]
    cprime = []
    dprime = []
    for k in range(levels):
        diag = jnp.ones_like(wet[0])
        if lower[k] is not None:
            diag = diag - lower[k]
        if upper[k] is not None:
            diag = diag - upper[k]
        if k == 0:
            denom = diag
            dval = tracer[:, 0] / denom
        else:
            denom = diag - lower[k] * cprime[k - 1]
            dval = (tracer[:, k] - lower[k] * dprime[k - 1]) / denom
        cprime.append(upper[k] / denom if upper[k] is not None else None)
        dprime.append(dval)
    result = [None] * levels
    result[levels - 1] = dprime[levels - 1]
    for k in range(levels - 2, -1, -1):
        result[k] = dprime[k] - cprime[k] * result[k + 1]
    return jnp.stack(result, axis=1)


def evolve(tracers, east_velocity, north_velocity, forcing, levels_wet, closure_in, closure_out):
    levels = tracers.shape[1]
    wet = (jnp.arange(levels, dtype=jnp.int32)[:, None, None] < levels_wet[None]).astype(jnp.float32)
    tracer = tracers * wet
    east_vel = east_velocity
    north_vel = north_velocity
    depth = levels_wet.astype(jnp.float32) / levels
    he_east = jnp.minimum(depth, jnp.roll(depth, -1, axis=1))
    he_west = jnp.roll(he_east, 1, axis=1)
    depth_pad = jnp.pad(depth, ((1, 1), (0, 0)))
    hn_north = jnp.minimum(depth, depth_pad[2:])
    hn_south = jnp.minimum(depth, depth_pad[:-2])
    centre_coef = SIG + he_east + he_west + hn_north + hn_south
    wet_east = jnp.roll(wet, -1, axis=2)
    wet_north = jnp.pad(wet, ((0, 0), (0, 1), (0, 0)))[:, 1:]

    def operate(field):
        rowpad = jnp.pad(field, ((1, 1), (0, 0)))
        return (centre_coef * field - he_east * jnp.roll(field, -1, axis=1) - he_west * jnp.roll(field, 1, axis=1)
                - hn_north * rowpad[2:] - hn_south * rowpad[:-2])

    surface = jnp.zeros_like(forcing)
    for step in range(STEPS):
        u_pad = periodic(east_vel, 2)
        wet_pad = periodic(wet, 2)
        for sub in range(SUB):
            tracer = advect(periodic(tracer, 2), u_pad, north_vel, wet_pad)
        tracer = closure_mix(tracer, wet, closure_in, closure_out)
        rhs = forcing + jnp.sum(tracer[0] - tracer[1], axis=0) / levels
        surface = jnp.zeros_like(rhs)
        residual = rhs
        direction = rhs
        norm_now = jnp.sum(residual * residual)
        for it in range(ITERS):
            image = operate(direction)
            alpha = norm_now / jnp.sum(direction * image)
            surface = surface + alpha * direction
            residual = residual - alpha * image
            norm_next = jnp.sum(residual * residual)
            direction = residual + (norm_next / norm_now) * direction
            norm_now = norm_next
        east_eta = jnp.roll(surface, -1, axis=1)
        north_eta = jnp.pad(surface, ((0, 1), (0, 0)))[1:]
        east_vel = east_vel - GRAV * (east_eta - surface)[None] * wet * wet_east
        north_vel = north_vel - GRAV * (north_eta - surface)[None] * wet * wet_north
    return tracer, surface


def reference(tracers, east_velocity, north_velocity, forcing, levels_wet, closure_in, closure_out):
    tracer, surface = evolve(tracers[0], east_velocity[0], north_velocity[0], forcing[0], levels_wet,
                             closure_in, closure_out)
    return tracer[None], surface[None]
```

```python
import functools

import jax
import jax.numpy as jnp
from jax import lax
from jax.experimental import pallas as pl
from jax.experimental.pallas import tpu as pltpu
from jax.sharding import PartitionSpec as P

STEPS = 3
SUB = 3
ITERS = 8
KMIN = 0.05
SIG = 0.1
GRAV = 0.1
ADV = 1.0 / 24.0

HALO = 8
OFF = 16
MESH = pl.DeviceIdType.MESH
F32 = jnp.float32


def roll(x, shift):
    return pltpu.roll(x, shift % 128, 1)


def kernel(n, tr_ref, u_ref, v_ref, fo_ref, lev_ref, cin_ref, w2_ref, out_ref, surf_ref,
           ta, tb, uu, vv, lv, fo, th, fl, w1, feat, score, cprime, dprime, gat, cc, he, hn, hs,
           xs, rs, ps, im, se, hsend, hrecv, gsend, grecv):
    levels, rows, cols = u_ref.shape
    width = cols + 2 * OFF
    chips = n // 2
    half = n // 2
    grid_rows = half * cols
    pad = 8
    me = lax.axis_index("lon")
    chip = me // 2
    core = me % 2
    right = lax.rem(me + 1, n)
    left = lax.rem(me + n - 1, n)
    sibling = 2 * chip + 1 - core

    lv[...] = jnp.zeros_like(lv)
    barrier = pltpu.get_barrier_semaphore()
    for d in range(1, n):
        pl.semaphore_signal(barrier, inc=1, device_id={"lon": lax.rem(me + d, n)}, device_id_type=MESH)

    lane = lax.broadcasted_iota(jnp.int32, (1, 2 * rows), 1)
    low = lane < rows
    south = lane % rows == 0
    north = lane % rows == rows - 1

    def transposed(top, bottom):
        return jnp.concatenate([top, bottom], axis=0).T

    def packed(x):
        a, b = x[: cols // 2], x[cols // 2 :]
        return jnp.where(low, a, b)

    def remote(src, dst, send, recv, where):
        return pltpu.make_async_remote_copy(src_ref=src, dst_ref=dst, send_sem=send, recv_sem=recv,
                                            device_id={"lon": where}, device_id_type=MESH)

    def halo_copies(kind, src, to_east, to_west):
        east = remote(src(OFF + cols - HALO), to_east, hsend.at[kind, 0], hrecv.at[kind, 0], right)
        west = remote(src(OFF), to_west, hsend.at[kind, 1], hrecv.at[kind, 1], left)
        return east, west

    def rows2(ref):
        return lambda start: ref.at[pl.ds(start, HALO), :]

    def rows3(ref):
        return lambda start: ref.at[:, pl.ds(start, HALO), :]

    def in_place(kind, view):
        return halo_copies(kind, view, view(OFF - HALO), view(OFF + cols))

    def tracer_halo(slot):
        return halo_copies(3 + slot, rows3(ta), th.at[slot, 0], th.at[slot, 1])

    def gather_copy(g, index, slot, where):
        return remote(gat.at[g, slot], gat.at[g, slot], gsend.at[g, index], grecv.at[g, index], where)

    def gather_start(g):
        gather_copy(g, 0, me, sibling).start()
        for d in range(1, chips):
            gather_copy(g, d, me, 2 * lax.rem(chip + d, chips) + core).start()

    def gather_finish(g):
        for d in range(1, chips):
            slot = 2 * lax.rem(chip + chips - d, chips) + core
            gather_copy(g, d, slot, sibling).wait_recv()
            gather_copy(g, chips + d, slot, sibling).start()
        gather_copy(g, 0, sibling, sibling).wait_recv()
        for d in range(1, chips):
            slot = 2 * lax.rem(chip + chips - d, chips) + 1 - core
            gather_copy(g, chips + d, slot, sibling).wait_recv()
        for d in range(0, 2 * chips):
            if d != chips:
                gather_copy(g, d, me, sibling).wait_send()

    def unpack_gathered(g, dst):
        def body(c, carry):
            a = gat[g, c]
            b = gat[g, c + half]
            base = pl.multiple_of(pad + c * cols, 8)
            dst[pl.ds(base, cols // 2), :] = jnp.where(low, a, roll(b, rows))
            dst[pl.ds(base + cols // 2, cols // 2), :] = jnp.where(low, roll(a, rows), b)
            return carry
        lax.fori_loop(0, half, body, 0)

    def wrap(ref):
        ref[0:pad, :] = roll(ref[grid_rows : grid_rows + pad, :], rows)
        ref[pad + grid_rows : pad + grid_rows + pad, :] = roll(ref[pad : 2 * pad, :], rows)

    own_lev = lev_ref[...].astype(F32)
    own_lev = transposed(own_lev, own_lev)
    lv[OFF : OFF + cols, :] = own_lev
    gat[0, me] = packed(own_lev)
    pl.semaphore_wait(barrier, n - 1)
    for copy in in_place(0, rows2(lv)):
        copy.start()
    gather_start(0)

    def load_level(k, carry):
        ta[k, OFF : OFF + cols, :] = jnp.where(
            own_lev > k.astype(F32), transposed(tr_ref[0, k], tr_ref[1, k]), 0.0)
        uk = u_ref[k]
        uu[k, OFF : OFF + cols, :] = transposed(uk, uk)
        vk = v_ref[k]
        vv[k, OFF : OFF + cols, :] = transposed(vk, vk)
        return carry
    lax.fori_loop(0, levels, load_level, 0)
    for copy in in_place(1, rows3(uu)) + in_place(2, rows3(vv)) + tracer_halo(0):
        copy.start()
    fo[...] = transposed(fo_ref[...], fo_ref[...])
    for m in range(4):
        w1[m] = jnp.broadcast_to(cin_ref[:, m : m + 1], w1.shape[1:])
    for copy in in_place(0, rows2(lv)) + in_place(1, rows3(uu)) + in_place(2, rows3(vv)):
        copy.wait()

    first, last = OFF - HALO, OFF + cols + HALO
    lev_mid = lv[first:last, :]
    lev_east = jnp.minimum(lev_mid, lv[first + 1 : last + 1, :])
    lev_north = jnp.minimum(lev_mid, jnp.where(north, 0.0, roll(lev_mid, -1)))
    se[1, first:last, :] = lev_east
    se[2, first:last, :] = lev_north

    def mask_level(k, carry):
        kf = k.astype(F32)
        uu[k, first:last, :] = jnp.where(se[1, first:last, :] > kf, uu[k, first:last, :] * ADV, 0.0)
        vv[k, first:last, :] = jnp.where(se[2, first:last, :] > kf, vv[k, first:last, :] * ADV, 0.0)
        return carry
    lax.fori_loop(0, levels, mask_level, 0)

    def flux(vel, tm1, t0, t1, t2):
        s = t0 + t1
        up = jnp.where(vel > 0, t0, t1)
        far = jnp.where(vel > 0, tm1, t2)
        return vel * ((s + s) + (3.0 * up - far))

    def advect(src, dst):
        block = 24

        def level(k, carry):
            for r in range(first, last, block):
                f = flux(uu[k, r : r + block, :], src[k, r - 1 : r - 1 + block, :], src[k, r : r + block, :],
                         src[k, r + 1 : r + 1 + block, :], src[k, r + 2 : r + 2 + block, :])
                fl[r : r + block, :] = f
            for r in range(first, last, block):
                t0 = src[k, r : r + block, :]
                tn = roll(t0, -1)
                ts = jnp.where(south, 0.0, roll(t0, 1))
                tnn = jnp.where(lane % rows == rows - 2, 0.0, roll(t0, -2))
                g = flux(vv[k, r : r + block, :], ts, t0, tn, tnn)
                zonal = fl[r : r + block, :] - fl[r - 1 : r - 1 + block, :]
                dst[k, r : r + block, :] = t0 - (zonal + (g - roll(g, 1)))
            return carry
        lax.fori_loop(0, levels, level, 0)

    w2 = w2_ref[...]
    w2_hi = w2.astype(jnp.bfloat16)
    w2_lo = (w2 - w2_hi.astype(F32)).astype(jnp.bfloat16)
    hid = w1.shape[1]
    w2_cat = jnp.where(lax.broadcasted_iota(jnp.int32, w2.shape, 1) < 2 * hid, w2_hi.astype(F32),
                       w2_lo.astype(F32)).astype(jnp.bfloat16)

    def mix(g):
        own = pl.ds(OFF, cols)
        for c in range(0, cols // 2, 32):
            a = pl.ds(OFF + c, 32)
            b = pl.ds(OFF + cols // 2 + c, 32)

            def total(ref, where):
                s = ref[0, where, :]
                for k in range(1, levels):
                    s = s + ref[k, where, :]
                return s * (1.0 / levels)
            for m, (x, y) in ((0, (tb[0, a, :], tb[0, b, :])), (2, (total(tb, a), total(tb, b)))):
                feat[m, c : c + 32, :] = jnp.where(low, x, roll(y, rows))
                feat[m + 1, c : c + 32, :] = jnp.where(low, roll(x, rows), y)

        group = 4

        def closure(i, carry):
            tiles_hi, tiles_lo = [], []
            for q in range(group):
                row = i * group + q
                acc = w1[0] * feat[0, pl.ds(row, 1), :]
                for m in range(1, 4):
                    acc = acc + w1[m] * feat[m, pl.ds(row, 1), :]
                h = jnp.tanh(acc)
                h_hi = h.astype(jnp.bfloat16)
                tiles_hi.append(h_hi)
                tiles_lo.append((h - h_hi.astype(F32)).astype(jnp.bfloat16))
            hi = jnp.concatenate(tiles_hi, axis=1)
            lo = jnp.concatenate(tiles_lo, axis=1)
            x = jnp.dot(w2_cat, jnp.concatenate([hi, lo, hi, lo], axis=0), preferred_element_type=F32)
            y = 2.0 * (KMIN + (jnp.maximum(x, 0.0) + jnp.log(1.0 + jnp.exp(-jnp.abs(x)))))
            for q in range(group):
                score[pl.ds(pl.multiple_of((i * group + q) * 16, 16), 16), :] = y[:, q * 128 : q * 128 + 128]
            return carry
        lax.fori_loop(0, cols // 2 // group, closure, 0)

        def columns(i, carry):
            start = (pl.multiple_of(OFF + i * 8, 8), pl.multiple_of(OFF + cols // 2 + i * 8, 8))
            lev = [lv[pl.ds(s, 8), :] for s in start]
            e = [[None, None] for _ in range(levels)]
            d = [[None, None] for _ in range(levels)]
            before = [None, None]
            for k in range(levels):
                if k < levels - 1:
                    p = score[pl.ds(i * 128 + k, 8, stride=16), :]
                    r = roll(p, rows)
                    kap = (jnp.where(low, p, r), jnp.where(low, r, p))
                for w in range(2):
                    t = tb[k, pl.ds(start[w], 8), :]
                    denom = 1.0
                    if k < levels - 1:
                        a = jnp.where(lev[w] > float(k + 1), kap[w], 0.0)
                        denom = denom + a
                    if k > 0:
                        denom = denom + before[w] * (1.0 - e[k - 1][w])
                        t = t + before[w] * d[k - 1][w]
                    inv = 1.0 / denom
                    d[k][w] = t * inv
                    if k < levels - 1:
                        e[k][w] = a * inv
                        before[w] = a
            for w in range(2):
                x = d[levels - 1][w]
                ta[levels - 1, pl.ds(start[w], 8), :] = x
                s = x
                for k in range(levels - 2, -1, -1):
                    x = d[k][w] + e[k][w] * x
                    ta[k, pl.ds(start[w], 8), :] = x
                    s = s + x
                diff = s - roll(s, rows)
                rhs = fo[pl.ds(start[w] - OFF, 8), :] + jnp.where(low, diff, -diff) * (1.0 / levels)
                se[0, pl.ds(start[w] - OFF, 8), :] = rhs
            return carry
        lax.fori_loop(0, cols // 16, columns, 0)
        gat[g, me] = packed(se[0, 0:cols, :])

    blocks = grid_rows // cols

    def spread(acc):
        acc = jnp.sum(acc.reshape(cols // 8, 8, 128), axis=0)
        return acc

    def total_of(acc):
        s = jnp.sum(jnp.sum(acc, axis=0, keepdims=True), axis=1, keepdims=True)
        return jnp.broadcast_to(s, (1, 128))

    def grid_loop(body):
        def step(b, acc):
            return acc + body(pl.multiple_of(pad + b * cols, 8))
        return total_of(lax.fori_loop(0, blocks, step, jnp.zeros((8, 128), F32)))

    def solve(g):
        unpack_gathered(g, rs)

        def init(r):
            where = pl.ds(r, cols)
            x = rs[where, :]
            ps[where, :] = x
            xs[where, :] = jnp.zeros_like(x)
            return spread(x * x)
        norm = grid_loop(init)
        wrap(ps)

        def iteration(it, norm):
            def image(r):
                where = pl.ds(r, cols)
                p = ps[where, :]
                y = (cc[where, :] * p - he[where, :] * ps[pl.ds(r + 1, cols), :]
                     - he[pl.ds(r - 1, cols), :] * ps[pl.ds(r - 1, cols), :]
                     - hn[where, :] * roll(p, -1) - hs[where, :] * roll(p, 1))
                im[where, :] = y
                return spread(p * y)
            alpha = norm / grid_loop(image)

            def update(r):
                where = pl.ds(r, cols)
                x = rs[where, :] - alpha * im[where, :]
                rs[where, :] = x
                xs[where, :] = xs[where, :] + alpha * ps[where, :]
                return spread(x * x)
            after = grid_loop(update)
            beta = after / norm

            def direct(b, carry):
                where = pl.ds(pl.multiple_of(pad + b * cols, 8), cols)
                ps[where, :] = rs[where, :] + beta * ps[where, :]
                return carry
            lax.fori_loop(0, blocks, direct, 0)
            wrap(ps)
            return after
        lax.fori_loop(0, ITERS, iteration, norm)
        wrap(xs)

    def coefficients():
        unpack_gathered(0, im)
        wrap(im)

        def faces(b, carry):
            r = pl.multiple_of(pad + b * cols, 8)
            where = pl.ds(r, cols)
            x = im[where, :] * (1.0 / levels)
            he[where, :] = jnp.minimum(x, im[pl.ds(r + 1, cols), :] * (1.0 / levels))
            y = jnp.minimum(x, jnp.where(north, 0.0, roll(x, -1)))
            hn[where, :] = y
            hs[where, :] = roll(y, 1)
            return carry
        lax.fori_loop(0, blocks, faces, 0)
        wrap(he)

        def centre(b, carry):
            r = pl.multiple_of(pad + b * cols, 8)
            where = pl.ds(r, cols)
            cc[where, :] = SIG + he[where, :] + he[pl.ds(r - 1, cols), :] + hn[where, :] + hs[where, :]
            return carry
        lax.fori_loop(0, blocks, centre, 0)

    side = low == (me < half)

    def own_surface():
        start = pl.multiple_of(lax.rem(me, half) * cols, 8)
        x = xs[pl.ds(start, cols + 2 * pad), :]
        se[0, first:last, :] = jnp.where(side, x, roll(x, rows))
        se[0, last : last + 8, :] = jnp.zeros((8, 128), F32)

    se[0] = jnp.zeros(se.shape[1:], F32)
    def step(s, carry):
        for copy in tracer_halo(s):
            copy.wait()

        def put(k, c):
            ta[k, first:OFF, :] = th[s, 0, k]
            ta[k, OFF + cols : last, :] = th[s, 1, k]
            return c
        lax.fori_loop(0, levels, put, 0)
        advect(ta, tb)
        advect(tb, ta)
        advect(ta, tb)
        mix(s + 1)
        gather_start(s + 1)

        @pl.when(s < STEPS - 1)
        def _():
            for copy in tracer_halo(s + 1):
                copy.start()

        @pl.when(s == 0)
        def _():
            gather_finish(0)
            coefficients()
        gather_finish(s + 1)
        solve(s + 1)
        own_surface()

        @pl.when(s < STEPS - 1)
        def _():
            mid = se[0, first:last, :]
            ge = (GRAV * ADV) * (se[0, first + 1 : last + 1, :] - mid)
            gn = (GRAV * ADV) * (jnp.where(north, 0.0, roll(mid, -1)) - mid)
            cprime[...] = ge
            dprime[...] = gn

            def velocity(k, c):
                kf = k.astype(F32)
                uu[k, first:last, :] = uu[k, first:last, :] - jnp.where(se[1, first:last, :] > kf, cprime[...], 0.0)
                vv[k, first:last, :] = vv[k, first:last, :] - jnp.where(se[2, first:last, :] > kf, dprime[...], 0.0)
                return c
            lax.fori_loop(0, levels, velocity, 0)
        return carry
    for ref in (ta, tb):
        def clear(k, c):
            ref[k, 0:first, :] = jnp.zeros((first, 128), F32)
            ref[k, last:width, :] = jnp.zeros((width - last, 128), F32)
            return c
        lax.fori_loop(0, levels, clear, 0)
    fl[0:first, :] = jnp.zeros((first, 128), F32)
    lax.fori_loop(0, STEPS, step, 0)

    def store_level(k, carry):
        x = ta[k, OFF : OFF + cols, :].T
        out_ref[0, k] = x[:rows]
        out_ref[1, k] = x[rows:]
        return carry
    lax.fori_loop(0, levels, store_level, 0)
    surf_ref[...] = se[0, OFF : OFF + cols, :].T[:rows]


def shards(n, tracers, east_velocity, north_velocity, forcing, levels_wet, closure_in, closure_out):
    _, _, levels, rows, cols = tracers.shape
    hid = closure_in.shape[0]
    width = cols + 2 * OFF
    span = cols + 2 * HALO
    grid_rows = (n // 2) * cols + 16
    w2 = jnp.pad(closure_out, ((0, 1), (0, 0)))
    w2 = jnp.concatenate([w2, w2, w2, w2], axis=1)
    lanes = 2 * rows
    whole = pl.BlockSpec(memory_space=pltpu.VMEM)
    vm = lambda *shape: pltpu.VMEM(shape, F32)
    tracer, surface = pl.pallas_call(
        functools.partial(kernel, n),
        out_shape=(jax.ShapeDtypeStruct(tracers.shape[1:], F32), jax.ShapeDtypeStruct((rows, cols), F32)),
        in_specs=[whole] * 7,
        out_specs=(whole, whole),
        scratch_shapes=[
            vm(levels, width, lanes), vm(levels, width, lanes), vm(levels, width, lanes), vm(levels, width, lanes),
            vm(width, lanes), vm(cols, lanes), vm(STEPS, 2, levels, HALO, lanes), vm(width, lanes),
            vm(4, hid, lanes), vm(4, cols // 2, lanes), vm(cols // 2 * 16, lanes),
            vm(span, lanes), vm(span, lanes),
            vm(STEPS + 1, n, cols // 2, lanes),
            vm(grid_rows, lanes), vm(grid_rows, lanes), vm(grid_rows, lanes), vm(grid_rows, lanes),
            vm(grid_rows, lanes), vm(grid_rows, lanes), vm(grid_rows, lanes), vm(grid_rows, lanes),
            vm(3, width, lanes),
            pltpu.SemaphoreType.DMA((3 + STEPS, 2)), pltpu.SemaphoreType.DMA((3 + STEPS, 2)),
            pltpu.SemaphoreType.DMA((STEPS + 1, n)), pltpu.SemaphoreType.DMA((STEPS + 1, n)),
        ],
        compiler_params=pltpu.CompilerParams(
            collective_id=0, has_side_effects=True, vmem_limit_bytes=56 * 1024 * 1024),
    )(tracers[0], east_velocity[0], north_velocity[0], forcing[0], levels_wet, closure_in, w2)
    return tracer[None], surface[None]


def solution(mesh):
    in_specs = (
        P("grp", None, None, None, "lon"),
        P("grp", None, None, "lon"),
        P("grp", None, None, "lon"),
        P("grp", None, "lon"),
        P(None, "lon"),
        P(),
        P(),
    )
    out_specs = (P("grp", None, None, None, "lon"), P("grp", None, "lon"))
    return jax.shard_map(functools.partial(shards, mesh.shape["lon"]), mesh=mesh, in_specs=in_specs,
                         out_specs=out_specs, check_vma=False)
```

```python
import functools

import jax
import jax.numpy as jnp
from jax import lax
from jax.experimental import pallas as pl
from jax.experimental.pallas import tpu as pltpu
from jax.sharding import PartitionSpec as P

STEPS = 3
SUB = 3
ITERS = 8
KMIN = 0.05
SIG = 0.1
GRAV = 0.1
ADV = 1.0 / 24.0

HALO = 8
OFF = 16
MESH = pl.DeviceIdType.MESH
F32 = jnp.float32


def roll(x, shift):
    return pltpu.roll(x, shift % 128, 1)


def kernel(n, tr_ref, u_ref, v_ref, fo_ref, lev_ref, cin_ref, w2_ref, out_ref, surf_ref,
           ta, tb, uu, vv, lv, fo, th, fl, w1, feat, score, cprime, dprime, gat, cc, he, hn, hs,
           xs, rs, ps, im, se, w2s, hsend, hrecv, gsend, grecv):
    levels, rows, cols = u_ref.shape
    width = cols + 2 * OFF
    half = n // 2
    grid_rows = half * cols
    pad = 8
    me = lax.axis_index("lon")
    chip = me // 2
    core = me % 2
    right = lax.rem(me + 1, n)
    left = lax.rem(me + n - 1, n)
    sibling = 2 * chip + 1 - core

    lv[...] = jnp.zeros_like(lv)
    barrier = pltpu.get_barrier_semaphore()
    for d in range(1, n):
        pl.semaphore_signal(barrier, inc=1, device_id={"lon": lax.rem(me + d, n)}, device_id_type=MESH)

    lane = lax.broadcasted_iota(jnp.int32, (1, 2 * rows), 1)
    low = lane < rows
    south = lane % rows == 0
    north = lane % rows == rows - 1

    def transposed(top, bottom):
        return jnp.concatenate([top, bottom], axis=0).T

    def packed(x):
        a, b = x[: cols // 2], x[cols // 2 :]
        return jnp.where(low, a, b)

    def remote(src, dst, send, recv, where):
        return pltpu.make_async_remote_copy(src_ref=src, dst_ref=dst, send_sem=send, recv_sem=recv,
                                            device_id={"lon": where}, device_id_type=MESH)

    def halo_copies(kind, src, to_east, to_west):
        east = remote(src(OFF + cols - HALO), to_east, hsend.at[kind, 0], hrecv.at[kind, 0], right)
        west = remote(src(OFF), to_west, hsend.at[kind, 1], hrecv.at[kind, 1], left)
        return east, west

    def rows2(ref):
        return lambda start: ref.at[pl.ds(start, HALO), :]

    def rows3(ref):
        return lambda start: ref.at[:, pl.ds(start, HALO), :]

    def in_place(kind, view):
        return halo_copies(kind, view, view(OFF - HALO), view(OFF + cols))

    def tracer_halo(slot):
        return halo_copies(3 + slot, rows3(ta), th.at[slot, 0], th.at[slot, 1])

    def gather_copy(g, index, slot, where):
        return remote(gat.at[g, slot], gat.at[g, slot], gsend.at[g, index], grecv.at[g, index], where)

    chips = n // 2

    def gather_start(g):
        gather_copy(g, 0, me, sibling).start()
        for d in range(1, chips):
            gather_copy(g, d, me, 2 * lax.rem(chip + d, chips) + core).start()

    def gather_finish(g):
        for d in range(1, chips):
            slot = 2 * lax.rem(chip + chips - d, chips) + core
            gather_copy(g, d, slot, sibling).wait_recv()
            gather_copy(g, chips + d, slot, sibling).start()
        gather_copy(g, 0, sibling, sibling).wait_recv()
        for d in range(1, chips):
            slot = 2 * lax.rem(chip + chips - d, chips) + 1 - core
            gather_copy(g, chips + d, slot, sibling).wait_recv()
        for d in range(0, 2 * chips):
            if d != chips:
                gather_copy(g, d, me, sibling).wait_send()

    def unpack_gathered(g, dst):
        def body(c, carry):
            a = gat[g, c]
            b = gat[g, c + half]
            base = pl.multiple_of(pad + c * cols, 8)
            dst[pl.ds(base, cols // 2), :] = jnp.where(low, a, roll(b, rows))
            dst[pl.ds(base + cols // 2, cols // 2), :] = jnp.where(low, roll(a, rows), b)
            return carry
        lax.fori_loop(0, half, body, 0)

    def wrap(ref):
        ref[0:pad, :] = roll(ref[grid_rows : grid_rows + pad, :], rows)
        ref[pad + grid_rows : pad + grid_rows + pad, :] = roll(ref[pad : 2 * pad, :], rows)

    own_lev = lev_ref[...].astype(F32)
    own_lev = transposed(own_lev, own_lev)
    lv[OFF : OFF + cols, :] = own_lev
    gat[0, me] = packed(own_lev)
    pl.semaphore_wait(barrier, n - 1)
    for copy in in_place(0, rows2(lv)):
        copy.start()
    gather_start(0)

    def load_level(k, carry):
        ta[k, OFF : OFF + cols, :] = jnp.where(
            own_lev > k.astype(F32), transposed(tr_ref[0, k], tr_ref[1, k]), 0.0)
        uk = u_ref[k]
        uu[k, OFF : OFF + cols, :] = transposed(uk, uk)
        vk = v_ref[k]
        vv[k, OFF : OFF + cols, :] = transposed(vk, vk)
        return carry
    lax.fori_loop(0, levels, load_level, 0)
    for copy in in_place(1, rows3(uu)) + in_place(2, rows3(vv)) + tracer_halo(0):
        copy.start()
    fo[...] = transposed(fo_ref[...], fo_ref[...])
    for m in range(4):
        w1[m] = jnp.broadcast_to(cin_ref[:, m : m + 1], w1.shape[1:])
    for copy in in_place(0, rows2(lv)) + in_place(1, rows3(uu)) + in_place(2, rows3(vv)):
        copy.wait()

    first, last = OFF - HALO, OFF + cols + HALO
    lev_mid = lv[first:last, :]
    lev_east = jnp.minimum(lev_mid, lv[first + 1 : last + 1, :])
    lev_north = jnp.minimum(lev_mid, jnp.where(north, 0.0, roll(lev_mid, -1)))
    se[1, first:last, :] = lev_east
    se[2, first:last, :] = lev_north

    def mask_level(k, carry):
        kf = k.astype(F32)
        uu[k, first:last, :] = jnp.where(se[1, first:last, :] > kf, uu[k, first:last, :] * ADV, 0.0)
        vv[k, first:last, :] = jnp.where(se[2, first:last, :] > kf, vv[k, first:last, :] * ADV, 0.0)
        return carry
    lax.fori_loop(0, levels, mask_level, 0)

    def flux(vel, tm1, t0, t1, t2):
        s = t0 + t1
        up = jnp.where(vel > 0, t0, t1)
        far = jnp.where(vel > 0, tm1, t2)
        return vel * ((s + s) + (3.0 * up - far))

    def advect(src, dst, margin):
        block = 24 if margin else 32
        lower, upper = OFF - margin, OFF + cols + margin

        def level(k, carry):
            for r in range(first, last, 24):
                f = flux(uu[k, r : r + 24, :], src[k, r - 1 : r - 1 + 24, :], src[k, r : r + 24, :],
                         src[k, r + 1 : r + 1 + 24, :], src[k, r + 2 : r + 2 + 24, :])
                fl[r : r + 24, :] = f
            for r in range(lower, upper, block):
                t0 = src[k, r : r + block, :]
                tn = roll(t0, -1)
                ts = jnp.where(south, 0.0, roll(t0, 1))
                tnn = jnp.where(lane % rows == rows - 2, 0.0, roll(t0, -2))
                g = flux(vv[k, r : r + block, :], ts, t0, tn, tnn)
                zonal = fl[r : r + block, :] - fl[r - 1 : r - 1 + block, :]
                dst[k, r : r + block, :] = t0 - (zonal + (g - roll(g, 1)))
            return carry
        lax.fori_loop(0, levels, level, 0, unroll=2)

    w2s[...] = jnp.zeros_like(w2s)
    w2s[0 : levels - 1, :] = w2_ref[...]
    w2 = jnp.concatenate([w2s[...]] * 4, axis=1)
    w2_hi = w2.astype(jnp.bfloat16)
    w2_lo = (w2 - w2_hi.astype(F32)).astype(jnp.bfloat16)
    hid = w1.shape[1]
    w2_cat = jnp.where(lax.broadcasted_iota(jnp.int32, w2.shape, 1) < 2 * hid, w2_hi.astype(F32),
                       w2_lo.astype(F32)).astype(jnp.bfloat16)

    def mix(g):
        own = pl.ds(OFF, cols)
        for c in range(0, cols // 2, 32):
            a = pl.ds(OFF + c, 32)
            b = pl.ds(OFF + cols // 2 + c, 32)

            def total(ref, where):
                s = ref[0, where, :]
                for k in range(1, levels):
                    s = s + ref[k, where, :]
                return s * (1.0 / levels)
            for m, (x, y) in ((0, (tb[0, a, :], tb[0, b, :])), (2, (total(tb, a), total(tb, b)))):
                feat[m, c : c + 32, :] = jnp.where(low, x, roll(y, rows))
                feat[m + 1, c : c + 32, :] = jnp.where(low, roll(x, rows), y)

        group = 4

        def closure(i, carry):
            tiles_hi, tiles_lo = [], []
            for q in range(group):
                row = i * group + q
                acc = w1[0] * feat[0, pl.ds(row, 1), :]
                for m in range(1, 4):
                    acc = acc + w1[m] * feat[m, pl.ds(row, 1), :]
                h = jnp.tanh(acc)
                h_hi = h.astype(jnp.bfloat16)
                tiles_hi.append(h_hi)
                tiles_lo.append((h - h_hi.astype(F32)).astype(jnp.bfloat16))
            hi = jnp.concatenate(tiles_hi, axis=1)
            lo = jnp.concatenate(tiles_lo, axis=1)
            x = jnp.dot(w2_cat, jnp.concatenate([hi, lo, hi, lo], axis=0), preferred_element_type=F32)
            y = 2.0 * (KMIN + (jnp.maximum(x, 0.0) + jnp.log(1.0 + jnp.exp(-jnp.abs(x)))))
            for q in range(group):
                score[pl.ds(pl.multiple_of((i * group + q) * 16, 16), 16), :] = y[:, q * 128 : q * 128 + 128]
            return carry
        lax.fori_loop(0, cols // 2 // group, closure, 0, unroll=2)

        def columns(i, carry):
            start = (pl.multiple_of(OFF + i * 8, 8), pl.multiple_of(OFF + cols // 2 + i * 8, 8))
            lev = [lv[pl.ds(s, 8), :] for s in start]
            e = [[None, None] for _ in range(levels)]
            d = [[None, None] for _ in range(levels)]
            before = [None, None]
            for k in range(levels):
                if k < levels - 1:
                    p = score[pl.ds(i * 128 + k, 8, stride=16), :]
                    r = roll(p, rows)
                    kap = (jnp.where(low, p, r), jnp.where(low, r, p))
                for w in range(2):
                    t = tb[k, pl.ds(start[w], 8), :]
                    denom = 1.0
                    if k < levels - 1:
                        a = jnp.where(lev[w] > float(k + 1), kap[w], 0.0)
                        denom = denom + a
                    if k > 0:
                        denom = denom + before[w] * (1.0 - e[k - 1][w])
                        t = t + before[w] * d[k - 1][w]
                    inv = 1.0 / denom
                    d[k][w] = t * inv
                    if k < levels - 1:
                        e[k][w] = a * inv
                        before[w] = a
            for w in range(2):
                x = d[levels - 1][w]
                ta[levels - 1, pl.ds(start[w], 8), :] = x
                s = x
                for k in range(levels - 2, -1, -1):
                    x = d[k][w] + e[k][w] * x
                    ta[k, pl.ds(start[w], 8), :] = x
                    s = s + x
                diff = s - roll(s, rows)
                rhs = fo[pl.ds(start[w] - OFF, 8), :] + jnp.where(low, diff, -diff) * (1.0 / levels)
                se[0, pl.ds(start[w] - OFF, 8), :] = rhs
            return carry
        lax.fori_loop(0, cols // 16, columns, 0, unroll=2)
        gat[g, me] = packed(se[0, 0:cols, :])

    blocks = grid_rows // cols

    def spread(acc):
        acc = jnp.sum(acc.reshape(cols // 8, 8, 128), axis=0)
        return acc

    def total_of(acc):
        s = jnp.sum(jnp.sum(acc, axis=0, keepdims=True), axis=1, keepdims=True)
        return jnp.broadcast_to(s, (1, 128))

    def grid_loop(body):
        def step(b, acc):
            return acc + body(pl.multiple_of(pad + b * cols, 8))
        return total_of(lax.fori_loop(0, blocks, step, jnp.zeros((8, 128), F32), unroll=True))

    def solve(g):
        unpack_gathered(g, rs)

        def init(r):
            where = pl.ds(r, cols)
            x = rs[where, :]
            ps[where, :] = x
            xs[where, :] = jnp.zeros_like(x)
            return spread(x * x)
        norm = grid_loop(init)
        wrap(ps)

        def iteration(it, norm):
            def image(r):
                where = pl.ds(r, cols)
                p = ps[where, :]
                y = (cc[where, :] * p - he[where, :] * ps[pl.ds(r + 1, cols), :]
                     - he[pl.ds(r - 1, cols), :] * ps[pl.ds(r - 1, cols), :]
                     - hn[where, :] * roll(p, -1) - hs[where, :] * roll(p, 1))
                im[where, :] = y
                return spread(p * y)
            alpha = norm / grid_loop(image)

            def update(r):
                where = pl.ds(r, cols)
                x = rs[where, :] - alpha * im[where, :]
                rs[where, :] = x
                xs[where, :] = xs[where, :] + alpha * ps[where, :]
                return spread(x * x)
            after = grid_loop(update)
            beta = after / norm

            def direct(b, carry):
                where = pl.ds(pl.multiple_of(pad + b * cols, 8), cols)
                ps[where, :] = rs[where, :] + beta * ps[where, :]
                return carry
            lax.fori_loop(0, blocks, direct, 0, unroll=True)
            wrap(ps)
            return after
        lax.fori_loop(0, ITERS, iteration, norm)
        wrap(xs)

    def coefficients():
        unpack_gathered(0, im)
        wrap(im)

        def faces(b, carry):
            r = pl.multiple_of(pad + b * cols, 8)
            where = pl.ds(r, cols)
            x = im[where, :] * (1.0 / levels)
            he[where, :] = jnp.minimum(x, im[pl.ds(r + 1, cols), :] * (1.0 / levels))
            y = jnp.minimum(x, jnp.where(north, 0.0, roll(x, -1)))
            hn[where, :] = y
            hs[where, :] = roll(y, 1)
            return carry
        lax.fori_loop(0, blocks, faces, 0)
        wrap(he)

        def centre(b, carry):
            r = pl.multiple_of(pad + b * cols, 8)
            where = pl.ds(r, cols)
            cc[where, :] = SIG + he[where, :] + he[pl.ds(r - 1, cols), :] + hn[where, :] + hs[where, :]
            return carry
        lax.fori_loop(0, blocks, centre, 0)

    side = low == (me < half)

    def own_surface():
        start = pl.multiple_of(lax.rem(me, half) * cols, 8)
        x = xs[pl.ds(start, cols + 2 * pad), :]
        se[0, first:last, :] = jnp.where(side, x, roll(x, rows))
        se[0, last : last + 8, :] = jnp.zeros((8, 128), F32)

    se[0] = jnp.zeros(se.shape[1:], F32)
    def step(s, carry):
        for copy in tracer_halo(s):
            copy.wait()

        def put(k, c):
            ta[k, first:OFF, :] = th[s, 0, k]
            ta[k, OFF + cols : last, :] = th[s, 1, k]
            return c
        lax.fori_loop(0, levels, put, 0)
        advect(ta, tb, HALO)
        advect(tb, ta, HALO)
        advect(ta, tb, 0)
        mix(s + 1)
        gather_start(s + 1)

        @pl.when(s < STEPS - 1)
        def _():
            for copy in tracer_halo(s + 1):
                copy.start()

        @pl.when(s == 0)
        def _():
            gather_finish(0)
            coefficients()
        gather_finish(s + 1)
        solve(s + 1)
        own_surface()

        @pl.when(s < STEPS - 1)
        def _():
            mid = se[0, first:last, :]
            ge = (GRAV * ADV) * (se[0, first + 1 : last + 1, :] - mid)
            gn = (GRAV * ADV) * (jnp.where(north, 0.0, roll(mid, -1)) - mid)
            cprime[...] = ge
            dprime[...] = gn

            def velocity(k, c):
                kf = k.astype(F32)
                uu[k, first:last, :] = uu[k, first:last, :] - jnp.where(se[1, first:last, :] > kf, cprime[...], 0.0)
                vv[k, first:last, :] = vv[k, first:last, :] - jnp.where(se[2, first:last, :] > kf, dprime[...], 0.0)
                return c
            lax.fori_loop(0, levels, velocity, 0)
        return carry
    for ref in (ta, tb):
        def clear(k, c):
            ref[k, 0:first, :] = jnp.zeros((first, 128), F32)
            ref[k, last:width, :] = jnp.zeros((width - last, 128), F32)
            return c
        lax.fori_loop(0, levels, clear, 0)
    fl[0:first, :] = jnp.zeros((first, 128), F32)
    lax.fori_loop(0, STEPS, step, 0)

    def store_level(k, carry):
        x = ta[k, OFF : OFF + cols, :].T
        out_ref[0, k] = x[:rows]
        out_ref[1, k] = x[rows:]
        return carry
    lax.fori_loop(0, levels, store_level, 0)
    surf_ref[...] = se[0, OFF : OFF + cols, :].T[:rows]


def shards(n, tracers, east_velocity, north_velocity, forcing, levels_wet, closure_in, closure_out):
    _, _, levels, rows, cols = tracers.shape
    hid = closure_in.shape[0]
    width = cols + 2 * OFF
    span = cols + 2 * HALO
    grid_rows = (n // 2) * cols + 16
    lanes = 2 * rows
    whole = pl.BlockSpec(memory_space=pltpu.VMEM)
    vm = lambda *shape: pltpu.VMEM(shape, F32)
    tracer, surface = pl.pallas_call(
        functools.partial(kernel, n),
        out_shape=(jax.ShapeDtypeStruct(tracers.shape[1:], F32), jax.ShapeDtypeStruct((rows, cols), F32)),
        in_specs=[whole] * 7,
        out_specs=(whole, whole),
        scratch_shapes=[
            vm(levels, width, lanes), vm(levels, width, lanes), vm(levels, width, lanes), vm(levels, width, lanes),
            vm(width, lanes), vm(cols, lanes), vm(STEPS, 2, levels, HALO, lanes), vm(width, lanes),
            vm(4, hid, lanes), vm(4, cols // 2, lanes), vm(cols // 2 * 16, lanes),
            vm(span, lanes), vm(span, lanes),
            vm(STEPS + 1, n, cols // 2, lanes),
            vm(grid_rows, lanes), vm(grid_rows, lanes), vm(grid_rows, lanes), vm(grid_rows, lanes),
            vm(grid_rows, lanes), vm(grid_rows, lanes), vm(grid_rows, lanes), vm(grid_rows, lanes),
            vm(3, width, lanes), vm(levels, hid),
            pltpu.SemaphoreType.DMA((3 + STEPS, 2)), pltpu.SemaphoreType.DMA((3 + STEPS, 2)),
            pltpu.SemaphoreType.DMA((STEPS + 1, n)), pltpu.SemaphoreType.DMA((STEPS + 1, n)),
        ],
        compiler_params=pltpu.CompilerParams(
            collective_id=0, has_side_effects=True, vmem_limit_bytes=56 * 1024 * 1024),
    )(tracers[0], east_velocity[0], north_velocity[0], forcing[0], levels_wet, closure_in, closure_out)
    return tracer[None], surface[None]


def solution(mesh):
    in_specs = (
        P("grp", None, None, None, "lon"),
        P("grp", None, None, "lon"),
        P("grp", None, None, "lon"),
        P("grp", None, "lon"),
        P(None, "lon"),
        P(),
        P(),
    )
    out_specs = (P("grp", None, None, None, "lon"), P("grp", None, "lon"))
    return jax.shard_map(functools.partial(shards, mesh.shape["lon"]), mesh=mesh, in_specs=in_specs,
                         out_specs=out_specs, check_vma=False)
```

```python
import functools

import jax
import jax.numpy as jnp
from jax import lax
from jax.experimental import pallas as pl
from jax.experimental.pallas import tpu as pltpu
from jax.sharding import PartitionSpec as P

STEPS = 3
SUB = 3
ITERS = 8
KMIN = 0.05
SIG = 0.1
GRAV = 0.1
ADV = 1.0 / 24.0

HALO = 8
OFF = 16
MESH = pl.DeviceIdType.MESH
F32 = jnp.float32


def roll(x, shift):
    return pltpu.roll(x, shift % 128, 1)


def kernel(n, tr_ref, u_ref, v_ref, fo_ref, lev_ref, cin_ref, w2_ref, out_ref, surf_ref,
           ta, tb, uu, vv, lv, fo, th, fl, w1, feat, score, cprime, dprime, gat, cc, he, hn, hs,
           xs, rs, ps, im, se, w2s, hsend, hrecv, gsend, grecv):
    levels, rows, cols = u_ref.shape
    width = cols + 2 * OFF
    half = n // 2
    grid_rows = half * cols
    pad = 8
    me = lax.axis_index("lon")
    chip = me // 2
    core = me % 2
    right = lax.rem(me + 1, n)
    left = lax.rem(me + n - 1, n)
    sibling = 2 * chip + 1 - core

    lv[...] = jnp.zeros_like(lv)
    barrier = pltpu.get_barrier_semaphore()
    for d in range(1, n):
        pl.semaphore_signal(barrier, inc=1, device_id={"lon": lax.rem(me + d, n)}, device_id_type=MESH)

    lane = lax.broadcasted_iota(jnp.int32, (1, 2 * rows), 1)
    low = lane < rows
    south = lane % rows == 0
    north = lane % rows == rows - 1

    def transposed(top, bottom):
        return jnp.concatenate([top, bottom], axis=0).T

    def packed(x):
        a, b = x[: cols // 2], x[cols // 2 :]
        return jnp.where(low, a, b)

    def remote(src, dst, send, recv, where):
        return pltpu.make_async_remote_copy(src_ref=src, dst_ref=dst, send_sem=send, recv_sem=recv,
                                            device_id={"lon": where}, device_id_type=MESH)

    def halo_copies(kind, src, to_east, to_west):
        east = remote(src(OFF + cols - HALO), to_east, hsend.at[kind, 0], hrecv.at[kind, 0], right)
        west = remote(src(OFF), to_west, hsend.at[kind, 1], hrecv.at[kind, 1], left)
        return east, west

    def rows2(ref):
        return lambda start: ref.at[pl.ds(start, HALO), :]

    def rows3(ref):
        return lambda start: ref.at[:, pl.ds(start, HALO), :]

    def in_place(kind, view):
        return halo_copies(kind, view, view(OFF - HALO), view(OFF + cols))

    def tracer_halo(slot):
        return halo_copies(3 + slot, rows3(ta), th.at[slot, 0], th.at[slot, 1])

    def gather_copy(g, index, slot, where):
        return remote(gat.at[g, slot], gat.at[g, slot], gsend.at[g, index], grecv.at[g, index], where)

    chips = n // 2

    def gather_start(g):
        gather_copy(g, 0, me, sibling).start()
        for d in range(1, chips):
            gather_copy(g, d, me, 2 * lax.rem(chip + d, chips) + core).start()

    def gather_finish(g):
        for d in range(1, chips):
            slot = 2 * lax.rem(chip + chips - d, chips) + core
            gather_copy(g, d, slot, sibling).wait_recv()
            gather_copy(g, chips + d, slot, sibling).start()
        gather_copy(g, 0, sibling, sibling).wait_recv()
        for d in range(1, chips):
            slot = 2 * lax.rem(chip + chips - d, chips) + 1 - core
            gather_copy(g, chips + d, slot, sibling).wait_recv()
        for d in range(0, 2 * chips):
            if d != chips:
                gather_copy(g, d, me, sibling).wait_send()

    def unpack_gathered(g, dst):
        def body(c, carry):
            a = gat[g, c]
            b = gat[g, c + half]
            base = pl.multiple_of(pad + c * cols, 8)
            dst[pl.ds(base, cols // 2), :] = jnp.where(low, a, roll(b, rows))
            dst[pl.ds(base + cols // 2, cols // 2), :] = jnp.where(low, roll(a, rows), b)
            return carry
        lax.fori_loop(0, half, body, 0, unroll=True)

    def wrap(ref):
        ref[0:pad, :] = roll(ref[grid_rows : grid_rows + pad, :], rows)
        ref[pad + grid_rows : pad + grid_rows + pad, :] = roll(ref[pad : 2 * pad, :], rows)

    own_lev = lev_ref[...].astype(F32)
    own_lev = transposed(own_lev, own_lev)
    lv[OFF : OFF + cols, :] = own_lev
    gat[0, me] = packed(own_lev)
    pl.semaphore_wait(barrier, n - 1)
    for copy in in_place(0, rows2(lv)):
        copy.start()
    gather_start(0)

    def load_level(k, carry):
        ta[k, OFF : OFF + cols, :] = jnp.where(
            own_lev > k.astype(F32), transposed(tr_ref[0, k], tr_ref[1, k]), 0.0)
        uk = u_ref[k]
        uu[k, OFF : OFF + cols, :] = transposed(uk, uk)
        vk = v_ref[k]
        vv[k, OFF : OFF + cols, :] = transposed(vk, vk)
        return carry
    lax.fori_loop(0, levels, load_level, 0, unroll=2)
    for copy in in_place(1, rows3(uu)) + in_place(2, rows3(vv)) + tracer_halo(0):
        copy.start()
    fo[...] = transposed(fo_ref[...], fo_ref[...])
    for m in range(4):
        w1[m] = jnp.broadcast_to(cin_ref[:, m : m + 1], w1.shape[1:])
    for copy in in_place(0, rows2(lv)) + in_place(1, rows3(uu)) + in_place(2, rows3(vv)):
        copy.wait()

    first, last = OFF - HALO, OFF + cols + HALO
    lev_mid = lv[first:last, :]
    lev_east = jnp.minimum(lev_mid, lv[first + 1 : last + 1, :])
    lev_north = jnp.minimum(lev_mid, jnp.where(north, 0.0, roll(lev_mid, -1)))
    se[1, first:last, :] = lev_east
    se[2, first:last, :] = lev_north

    def mask_level(k, carry):
        kf = k.astype(F32)
        uu[k, first:last, :] = jnp.where(se[1, first:last, :] > kf, uu[k, first:last, :] * ADV, 0.0)
        vv[k, first:last, :] = jnp.where(se[2, first:last, :] > kf, vv[k, first:last, :] * ADV, 0.0)
        return carry
    lax.fori_loop(0, levels, mask_level, 0, unroll=2)

    def flux(vel, tm1, t0, t1, t2):
        s = t0 + t1
        up = jnp.where(vel > 0, t0, t1)
        far = jnp.where(vel > 0, tm1, t2)
        return vel * ((s + s) + (3.0 * up - far))

    def advect(src, dst, margin):
        block = 24 if margin else 32
        lower, upper = OFF - margin, OFF + cols + margin

        def level(k, carry):
            for r in range(first, last, 24):
                f = flux(uu[k, r : r + 24, :], src[k, r - 1 : r - 1 + 24, :], src[k, r : r + 24, :],
                         src[k, r + 1 : r + 1 + 24, :], src[k, r + 2 : r + 2 + 24, :])
                fl[r : r + 24, :] = f
            for r in range(lower, upper, block):
                t0 = src[k, r : r + block, :]
                tn = roll(t0, -1)
                ts = jnp.where(south, 0.0, roll(t0, 1))
                tnn = jnp.where(lane % rows == rows - 2, 0.0, roll(t0, -2))
                g = flux(vv[k, r : r + block, :], ts, t0, tn, tnn)
                zonal = fl[r : r + block, :] - fl[r - 1 : r - 1 + block, :]
                dst[k, r : r + block, :] = t0 - (zonal + (g - roll(g, 1)))
            return carry
        lax.fori_loop(0, levels, level, 0, unroll=2)

    w2s[...] = jnp.zeros_like(w2s)
    w2s[0 : levels - 1, :] = w2_ref[...]
    w2 = jnp.concatenate([w2s[...]] * 4, axis=1)
    w2_hi = w2.astype(jnp.bfloat16)
    w2_lo = (w2 - w2_hi.astype(F32)).astype(jnp.bfloat16)
    hid = w1.shape[1]
    w2_cat = jnp.where(lax.broadcasted_iota(jnp.int32, w2.shape, 1) < 2 * hid, w2_hi.astype(F32),
                       w2_lo.astype(F32)).astype(jnp.bfloat16)

    def mix(g):
        own = pl.ds(OFF, cols)
        for c in range(0, cols // 2, 32):
            a = pl.ds(OFF + c, 32)
            b = pl.ds(OFF + cols // 2 + c, 32)

            def total(ref, where):
                s = ref[0, where, :]
                for k in range(1, levels):
                    s = s + ref[k, where, :]
                return s * (1.0 / levels)
            for m, (x, y) in ((0, (tb[0, a, :], tb[0, b, :])), (2, (total(tb, a), total(tb, b)))):
                feat[m, c : c + 32, :] = jnp.where(low, x, roll(y, rows))
                feat[m + 1, c : c + 32, :] = jnp.where(low, roll(x, rows), y)

        group = 4

        def closure(i, carry):
            tiles_hi, tiles_lo = [], []
            for q in range(group):
                row = i * group + q
                acc = w1[0] * feat[0, pl.ds(row, 1), :]
                for m in range(1, 4):
                    acc = acc + w1[m] * feat[m, pl.ds(row, 1), :]
                h = jnp.tanh(acc)
                h_hi = h.astype(jnp.bfloat16)
                tiles_hi.append(h_hi)
                tiles_lo.append((h - h_hi.astype(F32)).astype(jnp.bfloat16))
            hi = jnp.concatenate(tiles_hi, axis=1)
            lo = jnp.concatenate(tiles_lo, axis=1)
            x = jnp.dot(w2_cat, jnp.concatenate([hi, lo, hi, lo], axis=0), preferred_element_type=F32)
            y = 2.0 * (KMIN + (jnp.maximum(x, 0.0) + jnp.log(1.0 + jnp.exp(-jnp.abs(x)))))
            for q in range(group):
                score[pl.ds(pl.multiple_of((i * group + q) * 16, 16), 16), :] = y[:, q * 128 : q * 128 + 128]
            return carry
        lax.fori_loop(0, cols // 2 // group, closure, 0, unroll=2)

        def columns(i, carry):
            start = (pl.multiple_of(OFF + i * 8, 8), pl.multiple_of(OFF + cols // 2 + i * 8, 8))
            lev = [lv[pl.ds(s, 8), :] for s in start]
            e = [[None, None] for _ in range(levels)]
            d = [[None, None] for _ in range(levels)]
            before = [None, None]
            for k in range(levels):
                if k < levels - 1:
                    p = score[pl.ds(i * 128 + k, 8, stride=16), :]
                    r = roll(p, rows)
                    kap = (jnp.where(low, p, r), jnp.where(low, r, p))
                for w in range(2):
                    t = tb[k, pl.ds(start[w], 8), :]
                    denom = 1.0
                    if k < levels - 1:
                        a = jnp.where(lev[w] > float(k + 1), kap[w], 0.0)
                        denom = denom + a
                    if k > 0:
                        denom = denom + before[w] * (1.0 - e[k - 1][w])
                        t = t + before[w] * d[k - 1][w]
                    inv = 1.0 / denom
                    d[k][w] = t * inv
                    if k < levels - 1:
                        e[k][w] = a * inv
                        before[w] = a
            for w in range(2):
                x = d[levels - 1][w]
                ta[levels - 1, pl.ds(start[w], 8), :] = x
                s = x
                for k in range(levels - 2, -1, -1):
                    x = d[k][w] + e[k][w] * x
                    ta[k, pl.ds(start[w], 8), :] = x
                    s = s + x
                diff = s - roll(s, rows)
                rhs = fo[pl.ds(start[w] - OFF, 8), :] + jnp.where(low, diff, -diff) * (1.0 / levels)
                se[0, pl.ds(start[w] - OFF, 8), :] = rhs
            return carry
        lax.fori_loop(0, cols // 16, columns, 0, unroll=2)
        gat[g, me] = packed(se[0, 0:cols, :])

    blocks = grid_rows // cols

    def spread(acc):
        acc = jnp.sum(acc.reshape(cols // 8, 8, 128), axis=0)
        return acc

    def total_of(acc):
        s = jnp.sum(jnp.sum(acc, axis=0, keepdims=True), axis=1, keepdims=True)
        return jnp.broadcast_to(s, (1, 128))

    def grid_loop(body):
        def step(b, acc):
            return acc + body(pl.multiple_of(pad + b * cols, 8))
        return total_of(lax.fori_loop(0, blocks, step, jnp.zeros((8, 128), F32), unroll=True))

    def solve(g):
        unpack_gathered(g, rs)

        def init(r):
            where = pl.ds(r, cols)
            x = rs[where, :]
            ps[where, :] = x
            xs[where, :] = jnp.zeros_like(x)
            return spread(x * x)
        norm = grid_loop(init)
        wrap(ps)

        def iteration(it, norm):
            def image(r):
                where = pl.ds(r, cols)
                p = ps[where, :]
                y = (cc[where, :] * p - he[where, :] * ps[pl.ds(r + 1, cols), :]
                     - he[pl.ds(r - 1, cols), :] * ps[pl.ds(r - 1, cols), :]
                     - hn[where, :] * roll(p, -1) - hs[where, :] * roll(p, 1))
                im[where, :] = y
                return spread(p * y)
            alpha = norm / grid_loop(image)

            def update(r):
                where = pl.ds(r, cols)
                x = rs[where, :] - alpha * im[where, :]
                rs[where, :] = x
                xs[where, :] = xs[where, :] + alpha * ps[where, :]
                return spread(x * x)
            after = grid_loop(update)
            beta = after / norm

            def direct(b, carry):
                where = pl.ds(pl.multiple_of(pad + b * cols, 8), cols)
                ps[where, :] = rs[where, :] + beta * ps[where, :]
                return carry
            lax.fori_loop(0, blocks, direct, 0, unroll=True)
            wrap(ps)
            return after
        lax.fori_loop(0, ITERS, iteration, norm)
        wrap(xs)

    def coefficients():
        unpack_gathered(0, im)
        wrap(im)

        def faces(b, carry):
            r = pl.multiple_of(pad + b * cols, 8)
            where = pl.ds(r, cols)
            x = im[where, :] * (1.0 / levels)
            he[where, :] = jnp.minimum(x, im[pl.ds(r + 1, cols), :] * (1.0 / levels))
            y = jnp.minimum(x, jnp.where(north, 0.0, roll(x, -1)))
            hn[where, :] = y
            hs[where, :] = roll(y, 1)
            return carry
        lax.fori_loop(0, blocks, faces, 0)
        wrap(he)

        def centre(b, carry):
            r = pl.multiple_of(pad + b * cols, 8)
            where = pl.ds(r, cols)
            cc[where, :] = SIG + he[where, :] + he[pl.ds(r - 1, cols), :] + hn[where, :] + hs[where, :]
            return carry
        lax.fori_loop(0, blocks, centre, 0)

    side = low == (me < half)

    def own_surface():
        start = pl.multiple_of(lax.rem(me, half) * cols, 8)
        x = xs[pl.ds(start, cols + 2 * pad), :]
        se[0, first:last, :] = jnp.where(side, x, roll(x, rows))
        se[0, last : last + 8, :] = jnp.zeros((8, 128), F32)

    se[0] = jnp.zeros(se.shape[1:], F32)
    def step(s, carry):
        for copy in tracer_halo(s):
            copy.wait()

        def put(k, c):
            ta[k, first:OFF, :] = th[s, 0, k]
            ta[k, OFF + cols : last, :] = th[s, 1, k]
            return c
        lax.fori_loop(0, levels, put, 0, unroll=4)
        advect(ta, tb, HALO)
        advect(tb, ta, HALO)
        advect(ta, tb, 0)
        mix(s + 1)
        gather_start(s + 1)

        @pl.when(s < STEPS - 1)
        def _():
            for copy in tracer_halo(s + 1):
                copy.start()

        @pl.when(s == 0)
        def _():
            gather_finish(0)
            coefficients()
        gather_finish(s + 1)
        solve(s + 1)
        own_surface()

        @pl.when(s < STEPS - 1)
        def _():
            mid = se[0, first:last, :]
            ge = (GRAV * ADV) * (se[0, first + 1 : last + 1, :] - mid)
            gn = (GRAV * ADV) * (jnp.where(north, 0.0, roll(mid, -1)) - mid)
            cprime[...] = ge
            dprime[...] = gn

            def velocity(k, c):
                kf = k.astype(F32)
                uu[k, first:last, :] = uu[k, first:last, :] - jnp.where(se[1, first:last, :] > kf, cprime[...], 0.0)
                vv[k, first:last, :] = vv[k, first:last, :] - jnp.where(se[2, first:last, :] > kf, dprime[...], 0.0)
                return c
            lax.fori_loop(0, levels, velocity, 0, unroll=2)
        return carry
    for ref in (ta, tb):
        def clear(k, c):
            ref[k, 0:first, :] = jnp.zeros((first, 128), F32)
            ref[k, last:width, :] = jnp.zeros((width - last, 128), F32)
            return c
        lax.fori_loop(0, levels, clear, 0)
    fl[0:first, :] = jnp.zeros((first, 128), F32)
    lax.fori_loop(0, STEPS, step, 0)

    def store_level(k, carry):
        x = ta[k, OFF : OFF + cols, :].T
        out_ref[0, k] = x[:rows]
        out_ref[1, k] = x[rows:]
        return carry
    lax.fori_loop(0, levels, store_level, 0, unroll=2)
    surf_ref[...] = se[0, OFF : OFF + cols, :].T[:rows]


def shards(n, tracers, east_velocity, north_velocity, forcing, levels_wet, closure_in, closure_out):
    _, _, levels, rows, cols = tracers.shape
    hid = closure_in.shape[0]
    width = cols + 2 * OFF
    span = cols + 2 * HALO
    grid_rows = (n // 2) * cols + 16
    lanes = 2 * rows
    whole = pl.BlockSpec(memory_space=pltpu.VMEM)
    vm = lambda *shape: pltpu.VMEM(shape, F32)
    tracer, surface = pl.pallas_call(
        functools.partial(kernel, n),
        out_shape=(jax.ShapeDtypeStruct(tracers.shape[1:], F32), jax.ShapeDtypeStruct((rows, cols), F32)),
        in_specs=[whole] * 7,
        out_specs=(whole, whole),
        scratch_shapes=[
            vm(levels, width, lanes), vm(levels, width, lanes), vm(levels, width, lanes), vm(levels, width, lanes),
            vm(width, lanes), vm(cols, lanes), vm(STEPS, 2, levels, HALO, lanes), vm(width, lanes),
            vm(4, hid, lanes), vm(4, cols // 2, lanes), vm(cols // 2 * 16, lanes),
            vm(span, lanes), vm(span, lanes),
            vm(STEPS + 1, n, cols // 2, lanes),
            vm(grid_rows, lanes), vm(grid_rows, lanes), vm(grid_rows, lanes), vm(grid_rows, lanes),
            vm(grid_rows, lanes), vm(grid_rows, lanes), vm(grid_rows, lanes), vm(grid_rows, lanes),
            vm(3, width, lanes), vm(levels, hid),
            pltpu.SemaphoreType.DMA((3 + STEPS, 2)), pltpu.SemaphoreType.DMA((3 + STEPS, 2)),
            pltpu.SemaphoreType.DMA((STEPS + 1, n)), pltpu.SemaphoreType.DMA((STEPS + 1, n)),
        ],
        compiler_params=pltpu.CompilerParams(
            collective_id=0, has_side_effects=True, vmem_limit_bytes=56 * 1024 * 1024),
    )(tracers[0], east_velocity[0], north_velocity[0], forcing[0], levels_wet, closure_in, closure_out)
    return tracer[None], surface[None]


def solution(mesh):
    in_specs = (
        P("grp", None, None, None, "lon"),
        P("grp", None, None, "lon"),
        P("grp", None, None, "lon"),
        P("grp", None, "lon"),
        P(None, "lon"),
        P(),
        P(),
    )
    out_specs = (P("grp", None, None, None, "lon"), P("grp", None, "lon"))
    return jax.shard_map(functools.partial(shards, mesh.shape["lon"]), mesh=mesh, in_specs=in_specs,
                         out_specs=out_specs, check_vma=False)
```
